256 devices in a mesh: dp: 64 (over y, z, core), mp: 4 (over x).
Axes of the slice: x: 4, y: 4, z: 8, core: 2. Of those that a mesh axis runs over, the one named last changes fastest.
Arguments:
- documents: bfloat16 [131072, 1024], P('dp', 'mp'), may hold values from -6 to 6
- assign: int32 [131072], P('dp'), may hold values from 0 to 4095, as said below
- quality: float32 [131072], P('dp'), may hold values from 0.1 to 1
- centroids: bfloat16 [4096, 1024], P('mp'), may hold values from -6 to 6
Outputs:
- distances: float32 [131072], P('dp')
- new_centroids: bfloat16 [4096, 1024], P('dp', 'mp')
- cluster_quality: float32 [4096], P('dp')
- inertia: float32 [], replicated
The draws below stay inside these ranges and needn't reach their ends.
Inputs may be any that keep to these rules, and one draw needn't show every extreme that they name: `assign`: call the clusters o * 64 to (o + 1) * 64 - 1 those of owner o. Among each run of 2048 documents held by one index of dp, at most 64 have clusters of any one owner, and one owner, the same for every index, gets exactly 64 of them from every index.
All inputs are finite; a program needn't handle non-finite values.
Results may differ from the reference program's by a relative error of at most 0.0044.
Values may be sent and summed in bfloat16 or wider, within the bound.
No kernel may reach another device: no remote copies, remote signals or barrier semaphores. Data moves between devices by JAX's collectives and lax.ppermute only.
A program may use at most 64 MiB of HBM per device.

```python
import math
import jax
import jax.numpy as jnp

D = 1024
K = 4096
ROWS_DEV = 2048
DOCS = 131072
N_DP = 64


def draw_assign(key, part):
    owned = K // N_DP
    capacity = max(2, 2 * ROWS_DEV // N_DP)
    common = jax.random.randint(jax.random.fold_in(key, 7), (), 0, N_DP).astype(jnp.int32)

    def one_device(index):
        subkey = jax.random.fold_in(key, index + 100)
        key_one, key_two, key_three = jax.random.split(subkey, 3)
        others = (jnp.arange((N_DP - 1) * capacity, dtype=jnp.int32) // capacity).astype(jnp.int32)
        others = jnp.where(others >= common, others + 1, others)
        mixed = jax.random.permutation(key_one, others)
        owners = jnp.concatenate([jnp.zeros((capacity,), jnp.int32) + common, mixed[:ROWS_DEV - capacity]])
        owners = jax.random.permutation(key_two, owners)
        inside = jax.random.randint(key_three, (ROWS_DEV,), 0, owned).astype(jnp.int32)
        return (owners * owned + inside).astype(jnp.int32)
    return jax.vmap(one_device)(jnp.arange(N_DP, dtype=jnp.int32)).reshape(-1)


def levels(own_key, extent, pieces, smallest, top_value):
    loudness, own = 1.0, jax.random.fold_in(own_key, 6)
    for dim, blocks in pieces:
        draws = jnp.exp(jax.random.uniform(jax.random.fold_in(own, dim), (blocks,), jnp.float32, smallest / len(pieces), top_value / len(pieces)))
        loudness = loudness * jnp.repeat(draws, extent[dim] // blocks).reshape([-1 if axis == dim else 1 for axis in range(len(extent))])
    return loudness


def bell_draw(stream_key, shape, deviation, bound, cuts=(), kind=jnp.bfloat16):
    drawn = deviation * jax.random.normal(stream_key, shape, jnp.float32)
    if cuts:
        drawn = drawn * levels(stream_key, shape, cuts, -0.22, 0.18)
    return jnp.clip(drawn, -bound, bound).astype(kind)


def setup_inputs(seed: int = 0) -> dict:
    key_list = jax.random.split(jax.random.key(seed), 5)
    return {
        "documents": bell_draw(key_list[0], (DOCS, D), 1.0, 6.0, ((0, 64), (1, 4))),
        "assign": draw_assign(jax.random.fold_in(key_list[4], 71), 0),
        "quality": jnp.clip(jnp.exp(math.log(1.0) - 2.3025851 * jax.random.uniform(key_list[2], (DOCS,), jnp.float32) ** levels(key_list[2], (DOCS,), ((0, 64),), -0.2, 0.2)), 0.1, 1.0),
        "centroids": bell_draw(key_list[3], (K, D), 1.0, 6.0, ((0, 4),)),
    }


def reference(documents, assign, quality, centroids):
    values = documents.astype(jnp.float32)
    picked = centroids[assign].astype(jnp.float32)
    diff = values - picked
    distances = jnp.sum(diff * diff, axis=1) / D
    inertia = jnp.sum(distances) / DOCS
    weight = quality.astype(jnp.bfloat16).astype(jnp.float32)
    sums = jax.ops.segment_sum(weight[:, None] * values, assign, num_segments=K)
    counts = jax.ops.segment_sum(jnp.ones_like(weight), assign, num_segments=K)
    mass = jax.ops.segment_sum(weight, assign, num_segments=K)
    new_centroids = ((sums + centroids.astype(jnp.float32)) / (mass + 1.0)[:, None]).astype(jnp.bfloat16)
    cluster_quality = mass / (counts + 1.0)
    return distances, new_centroids, cluster_quality, inertia
```

```python
import jax
import jax.numpy as jnp
from jax import lax
from jax.experimental import pallas as pl
from jax.experimental.pallas import tpu as pltpu
from jax.sharding import Mesh, PartitionSpec as P

D = 1024
F32 = jnp.float32
BF16 = jnp.bfloat16
TILE = 256
LANES = 128


def all_to_all(x, axes):
    return lax.all_to_all(x, axes, split_axis=0, concat_axis=0, tiled=True)


def scatter_kernel(own_aux, own_docs, oth_aux, oth_docs, sums, hist):
    rows = own_docs.shape[0]
    tiles = sums.shape[0] // TILE
    sub = lax.broadcasted_iota(jnp.int32, (TILE, LANES), 0).astype(F32).astype(BF16)
    sides = ((own_aux, own_docs), (oth_aux, oth_docs))

    def cluster_tile(t, carry):
        total = jnp.zeros((TILE, own_docs.shape[1]), F32)
        base = (t * TILE).astype(F32)
        for aux, docs in sides:
            rel = jnp.clip(aux[0] - base, -1.0, float(TILE)).astype(BF16)
            weight = aux[1].astype(BF16)
            hot = jnp.concatenate(
                [
                    jnp.where(
                        sub == jnp.broadcast_to(rel[r : r + 1], (TILE, LANES)),
                        jnp.broadcast_to(weight[r : r + 1], (TILE, LANES)),
                        jnp.zeros((TILE, LANES), BF16),
                    )
                    for r in range(rows // LANES)
                ],
                axis=1,
            )
            total = total + jnp.dot(hot, docs[...], preferred_element_type=F32)
        sums[pl.ds(pl.multiple_of(t * TILE, TILE), TILE), :] = total.astype(BF16)
        return carry

    lax.fori_loop(0, tiles, cluster_tile, 0)

    owners = hist.shape[0]
    share = hist.shape[1] // 2
    owner_sub = lax.broadcasted_iota(jnp.int32, (owners, LANES), 0).astype(F32)
    local_sub = lax.broadcasted_iota(jnp.int32, (share, LANES), 0).astype(F32)
    total = jnp.zeros(hist.shape, F32)
    for aux, docs in sides:
        label = aux[0]
        owner = jnp.floor(label * (1.0 / share))
        local = label - owner * share
        weight = aux[1]
        owner_hot, local_hot = [], []
        for r in range(rows // LANES):
            owner_hot.append((owner_sub == owner[r : r + 1]).astype(F32))
            same = local_sub == local[r : r + 1]
            local_hot.append(
                jnp.concatenate(
                    [same.astype(F32), jnp.where(same, weight[r : r + 1], 0.0)], axis=0
                )
            )
        total = total + lax.dot_general(
            jnp.concatenate(owner_hot, axis=1).astype(BF16),
            jnp.concatenate(local_hot, axis=1).astype(BF16),
            (((1,), (1,)), ((), ())),
            preferred_element_type=F32,
        )
    hist[...] = total


def distance_kernel(core, own_aux, own_docs, oth_aux, oth_docs, table, out):
    rows = own_docs.shape[0]
    clusters = table.shape[0]
    lane = lax.broadcasted_iota(jnp.int32, (TILE, TILE), 1).astype(F32).astype(BF16)
    me = core[0]
    per = TILE // LANES
    total = jnp.zeros((1, LANES), F32)
    for side, (aux, docs) in enumerate(((own_aux, own_docs), (oth_aux, oth_docs))):
        where_to = me if side == 0 else 1 - me

        def doc_tile(i, total):
            columns = []
            for j in range(per):
                label = aux[0, pl.ds(i * per + j, 1), :]
                columns.append(jnp.broadcast_to(label, (LANES, LANES)).T)
            column = jnp.concatenate(columns, axis=0)
            high = jnp.floor(column * (1.0 / TILE))
            low = (column - high * TILE).astype(BF16)
            high = high.astype(BF16)
            same = jnp.concatenate([low, low], axis=1) == lane
            hots = []
            for t in range(clusters // TILE):
                hit = jnp.where(
                    high == jnp.full((TILE, LANES), t, BF16),
                    jnp.ones((TILE, LANES), BF16),
                    jnp.zeros((TILE, LANES), BF16),
                )
                hots.append(
                    jnp.where(
                        same, jnp.concatenate([hit, hit], axis=1), jnp.zeros((TILE, TILE), BF16)
                    )
                )
            hot = jnp.concatenate(hots, axis=1)
            picked = jnp.dot(hot, table[...], preferred_element_type=F32)
            start = pl.multiple_of(i * TILE, TILE)
            diff = docs[pl.ds(start, TILE), :].astype(F32) - picked
            square = diff * diff
            folded = square[:, :LANES]
            for k in range(1, square.shape[1] // LANES):
                folded = folded + square[:, k * LANES : (k + 1) * LANES]
            for j in range(per):
                row = jnp.sum(folded[j * LANES : (j + 1) * LANES].T, axis=0, keepdims=True)
                row = jnp.where(aux[0, pl.ds(i * per + j, 1), :] >= 0.0, row, 0.0)
                out[where_to, 0, pl.ds(i * per + j, 1), :] = row
                total = total + row
            return total

        total = lax.fori_loop(0, rows // TILE, doc_tile, total)
    docs_rows = rows // LANES
    for c in range(2):
        out[c, 0, pl.ds(docs_rows, out.shape[2] - docs_rows), :] = jnp.broadcast_to(
            total, (out.shape[2] - docs_rows, LANES)
        )
    for c in range(2):
        for m in range(1, out.shape[1]):
            out[c, m] = out[c, 0]


def update_kernel(recv, tail, old, centroids, quality, inertia):
    share = old.shape[0]
    totals = jnp.sum(tail[...], axis=0)
    counts = totals[0:1, 0:share]
    mass = totals[0:1, share : 2 * share]
    quality[...] = mass / (counts + 1.0)
    inertia[...] = jnp.broadcast_to(
        jnp.sum(totals[1:2, :], axis=1, keepdims=True), inertia.shape
    )
    sums = recv[0].astype(F32)
    for p in range(1, recv.shape[0]):
        sums = sums + recv[p].astype(F32)
    wide = jnp.broadcast_to(totals[0:1, :], (LANES, LANES)).T[share : 2 * share]
    divisor = jnp.concatenate([wide] * (old.shape[1] // LANES), axis=1) + 1.0
    centroids[...] = ((sums + old[...].astype(F32)) / divisor).astype(BF16)


def per_device(documents, assign, quality, centroids):
    rows, width = documents.shape
    core = lax.axis_index("c")
    n_mp = lax.axis_size("mp")
    n_yz = lax.axis_size("y") * lax.axis_size("z")
    clusters = centroids.shape[0] * n_mp
    share = clusters // (2 * n_yz)
    half = clusters // 2
    groups = rows // LANES
    params = pltpu.CompilerParams(vmem_limit_bytes=32 * 1024 * 1024)

    oth_docs = lax.ppermute(documents, "c", [(0, 1), (1, 0)])
    owner = assign // share
    label = (owner // 2) * share + assign % share
    weight = quality.astype(BF16).astype(F32).reshape(groups, LANES)
    own_label = jnp.where(owner % 2 == core, label, -1).astype(F32).reshape(groups, LANES)
    oth_label = jnp.where(owner % 2 == core, -1, label).astype(F32).reshape(groups, LANES)
    own_aux = jnp.stack([own_label, weight])
    oth_aux = lax.ppermute(jnp.stack([oth_label, weight]), "c", [(0, 1), (1, 0)])

    block = centroids.reshape(-1, 2, share, n_mp, width)
    block = lax.dynamic_index_in_dim(block, core, 1, keepdims=False)
    block = block.transpose(2, 0, 1, 3).reshape(n_mp, half // n_mp, width)
    table = all_to_all(block, "mp").reshape(half, width)

    sums, hist = pl.pallas_call(
        scatter_kernel,
        out_shape=(
            jax.ShapeDtypeStruct((half, width), BF16),
            jax.ShapeDtypeStruct((n_yz, 2 * share), F32),
        ),
        compiler_params=params,
        cost_estimate=pl.CostEstimate(
            flops=4 * rows * half * width, bytes_accessed=3 * rows * width * 2, transcendentals=0
        ),
        name="scatter",
    )(own_aux, documents, oth_aux, oth_docs)
    recv = all_to_all(sums.reshape(n_yz, share, width), ("y", "z"))

    pieces = pl.pallas_call(
        distance_kernel,
        out_shape=jax.ShapeDtypeStruct((2, n_mp, groups + 8, LANES), F32),
        in_specs=[pl.BlockSpec(memory_space=pltpu.SMEM)]
        + [pl.BlockSpec(memory_space=pltpu.VMEM)] * 5,
        compiler_params=params,
        cost_estimate=pl.CostEstimate(
            flops=4 * rows * half * width, bytes_accessed=3 * rows * width * 2, transcendentals=0
        ),
        name="distances",
    )(core.astype(jnp.int32).reshape(1), own_aux, documents, oth_aux, oth_docs, table)
    arrived = all_to_all(pieces.reshape(2 * n_mp, groups + 8, LANES), ("c", "mp"))
    arrived = jnp.sum(arrived, axis=0)
    distances = (arrived[:groups] / D).reshape(rows)

    total_docs = rows * n_yz * 2
    row = arrived[groups : groups + 1] / D / total_docs
    tail = jnp.concatenate(
        [hist.reshape(n_yz, 1, LANES), jnp.broadcast_to(row[None], (n_yz, 1, LANES))], axis=1
    )
    tail = jnp.pad(tail, ((0, 0), (0, 6), (0, 0)))
    tail = all_to_all(tail, ("y", "z"))

    first = (lax.axis_index("y") * lax.axis_size("z") + lax.axis_index("z")) * share
    old = lax.dynamic_slice_in_dim(table, first, share, 0)
    new_centroids, cluster_quality, inertia = pl.pallas_call(
        update_kernel,
        out_shape=(
            jax.ShapeDtypeStruct((share, width), BF16),
            jax.ShapeDtypeStruct((1, share), F32),
            jax.ShapeDtypeStruct((1, LANES), F32),
        ),
        compiler_params=params,
        name="update",
    )(recv, tail, old)
    return distances, new_centroids, cluster_quality.reshape(share), inertia[0, 0]


def solution(mesh):
    n_dp, n_mp = mesh.devices.shape
    n_y, n_z = 4, n_dp // 8
    fine = Mesh(mesh.devices.reshape(n_y, n_z, 2, n_mp), ("y", "z", "c", "mp"))
    dp = ("y", "z", "c")
    return jax.shard_map(
        per_device,
        mesh=fine,
        in_specs=(P(dp, "mp"), P(dp), P(dp), P("mp", None)),
        out_specs=(P(dp), P(dp, "mp"), P(dp), P()),
        check_vma=False,
    )
```

```python
import jax
import jax.numpy as jnp
from jax import lax
from jax.experimental import pallas as pl
from jax.experimental.pallas import tpu as pltpu
from jax.sharding import Mesh, PartitionSpec as P

D = 1024
F32 = jnp.float32
BF16 = jnp.bfloat16
TILE = 256
DOCS = 512
EXTRA = 16
NEAR = (0, 1, 3)
FAR = (2,)
LANES = 128
VMEM = pl.BlockSpec(memory_space=pltpu.VMEM)
SMEM = pl.BlockSpec(memory_space=pltpu.SMEM)
ANY = pl.BlockSpec(memory_space=pl.ANY)


def all_to_all(x, axes):
    return lax.all_to_all(x, axes, split_axis=0, concat_axis=0, tiled=True)


def shifted(x, axis, step):
    size = lax.axis_size(axis)
    return lax.ppermute(x, axis, [(i, (i + step) % size) for i in range(size)])


def cost(flops, moved):
    return pl.CostEstimate(flops=flops, bytes_accessed=moved, transcendentals=0)


def split3(x):
    one = x.astype(BF16)
    rest = x - one.astype(F32)
    two = rest.astype(BF16)
    three = (rest - two.astype(F32)).astype(BF16)
    return one.astype(F32), two.astype(F32), three.astype(F32)


def prep_kernel(assign, quality, cents, own_aux, oth_aux, *outs_and_scratch):
    outs, (label_in, weight_in, block, sems) = outs_and_scratch[:-4], outs_and_scratch[-4:]
    core, me = lax.axis_index("c"), lax.axis_index("mp")
    parts = len(outs)
    share, width = outs[0].shape[1], outs[0].shape[2]
    blocks = block.shape[0]
    copies = [
        pltpu.make_async_copy(cents.at[i, core], block.at[i], sems.at[i]) for i in range(blocks)
    ]
    small = [
        pltpu.make_async_copy(assign, label_in, sems.at[blocks]),
        pltpu.make_async_copy(quality, weight_in, sems.at[blocks + 1]),
    ]
    for copy in small + copies:
        copy.start()
    for copy in small:
        copy.wait()
    label = label_in[...]
    owner = lax.shift_right_logical(label, share.bit_length() - 1)
    local = lax.bitwise_and(label, share - 1)
    half = lax.shift_right_logical(owner, 1) * share + local
    side = lax.bitwise_and(owner, 1)
    weight = weight_in[...].astype(BF16).astype(F32)
    own_aux[0] = jnp.where(side == core, half, -1).astype(F32)
    own_aux[1] = weight
    oth_aux[0] = jnp.where(side == core, -1, half).astype(F32)
    oth_aux[1] = weight
    for i, copy in enumerate(copies):
        copy.wait()
        for s in range(parts):
            to = lax.rem(me + s, parts)
            columns = pl.ds(pl.multiple_of(to * width, width), width)
            outs[s][i] = block[i, :, columns]


def scatter_kernel(own_aux, own_docs, oth_aux, oth_docs, own_sums, *sums):
    rows = own_docs.shape[0]
    quarters = len(sums) + 1
    step = own_sums.shape[0] - EXTRA
    sub = lax.broadcasted_iota(jnp.int32, (TILE, LANES), 0).astype(F32).astype(BF16)
    y = lax.axis_index("y")
    sides = []
    for aux, docs in ((own_aux, own_docs), (oth_aux, oth_docs)):
        label = aux[0].astype(jnp.int32)
        shift = lax.bitwise_and(
            lax.shift_right_arithmetic(label, step.bit_length() - 1) - y, quarters - 1
        )
        moved = jnp.where(label < 0, -1, shift * step + lax.bitwise_and(label, step - 1))
        sides.append((moved.astype(F32), aux[1], docs))

    order = list(range(1, quarters)) + [0]
    for q in order:
        out = own_sums if q == 0 else sums[q - 1]
        for t in range(step // TILE):
            base = float(q * step + t * TILE)
            total = jnp.zeros((TILE, own_docs.shape[1]), F32)
            for label, weight, docs in sides:
                rel = jnp.clip(label - base, -1.0, float(TILE)).astype(BF16)
                weight = weight.astype(BF16)
                hot = jnp.concatenate(
                    [
                        jnp.where(
                            sub == jnp.broadcast_to(rel[r : r + 1], (TILE, LANES)),
                            jnp.broadcast_to(weight[r : r + 1], (TILE, LANES)),
                            jnp.zeros((TILE, LANES), BF16),
                        )
                        for r in range(rows // LANES)
                    ],
                    axis=1,
                )
                total = total + jnp.dot(hot, docs[...], preferred_element_type=F32)
            out[t * TILE : (t + 1) * TILE, :] = total.astype(out.dtype)

    share = own_docs.shape[1] // 4
    owners = quarters * step // share
    owner_sub = lax.broadcasted_iota(jnp.int32, (owners, LANES), 0).astype(F32)
    local_sub = lax.broadcasted_iota(jnp.int32, (share, LANES), 0).astype(F32)
    total = jnp.zeros((owners, 2 * share), F32)
    for label, weight, docs in sides:
        owner = jnp.floor(label * (1.0 / share))
        local = label - owner * share
        owner_hot, local_hot = [], []
        for r in range(rows // LANES):
            owner_hot.append((owner_sub == owner[r : r + 1]).astype(F32))
            same = local_sub == local[r : r + 1]
            local_hot.append(
                jnp.concatenate(
                    [same.astype(F32), jnp.where(same, weight[r : r + 1], 0.0)], axis=0
                )
            )
        total = total + lax.dot_general(
            jnp.concatenate(owner_hot, axis=1).astype(BF16),
            jnp.concatenate(local_hot, axis=1).astype(BF16),
            (((1,), (1,)), ((), ())),
            preferred_element_type=F32,
        )
    packed = jnp.concatenate([total[:, :share], *split3(total[:, share:])], axis=1)
    per = owners // quarters
    for q in order:
        out = own_sums if q == 0 else sums[q - 1]
        piece = packed[q * per : (q + 1) * per]
        pad = jnp.zeros((EXTRA - per, piece.shape[1]), F32)
        out[step:, :] = jnp.concatenate([piece, pad], axis=0).astype(out.dtype)


def squares(label, row_in, docs, tables, shifts):
    step = tables[0].shape[0]
    rows = docs.shape[0]
    per = DOCS // LANES
    parts = lax.axis_size("mp")
    lane = lax.broadcasted_iota(jnp.int32, (DOCS, TILE), 1).astype(F32).astype(BF16)
    shift = lax.bitwise_and(
        lax.axis_index("mp") - lax.shift_right_arithmetic(label, step.bit_length() - 1),
        parts - 1,
    )
    moved = jnp.full(label.shape, -1, jnp.int32)
    for k, s in enumerate(shifts):
        moved = jnp.where(shift == s, k * step + lax.bitwise_and(label, step - 1), moved)
    moved = jnp.where(label < 0, -1, moved).astype(F32)
    result = []
    for i in range(rows // DOCS):
        columns = []
        for j in range(per):
            row = moved[i * per + j : i * per + j + 1]
            columns.append(jnp.broadcast_to(row, (LANES, LANES)).T)
        column = jnp.concatenate(columns, axis=0)
        high = jnp.floor(column * (1.0 / TILE))
        low = (column - high * TILE).astype(BF16)
        high = high.astype(BF16)
        same = jnp.concatenate([low, low], axis=1) == lane
        picked = jnp.zeros((DOCS, docs.shape[1]), F32)
        for k, table in enumerate(tables):
            hots = []
            for t in range(step // TILE):
                hit = jnp.where(
                    high == jnp.full((DOCS, LANES), k * (step // TILE) + t, BF16),
                    jnp.ones((DOCS, LANES), BF16),
                    jnp.zeros((DOCS, LANES), BF16),
                )
                hots.append(
                    jnp.where(
                        same, jnp.concatenate([hit, hit], axis=1), jnp.zeros((DOCS, TILE), BF16)
                    )
                )
            picked = picked + jnp.dot(
                jnp.concatenate(hots, axis=1), table[...], preferred_element_type=F32
            )
        diff = docs[i * DOCS : (i + 1) * DOCS, :].astype(F32) - picked
        square = diff * diff
        folded = square[:, :LANES]
        for k in range(1, square.shape[1] // LANES):
            folded = folded + square[:, k * LANES : (k + 1) * LANES]
        for j in range(per):
            g = i * per + j
            row = jnp.sum(folded[j * LANES : (j + 1) * LANES].T, axis=0, keepdims=True)
            other = 0.0 if row_in is None else row_in[g : g + 1, :]
            result.append(jnp.where(moved[g : g + 1] >= 0.0, row, other))
    return result


def near_kernel(own_aux, own_docs, oth_aux, oth_docs, *rest):
    tables, outs = rest[:-2], rest[-2:]
    for aux, docs, out in ((own_aux, own_docs, outs[0]), (oth_aux, oth_docs, outs[1])):
        label = aux[0].astype(jnp.int32)
        for g, row in enumerate(squares(label, None, docs, tables, NEAR)):
            out[g : g + 1, :] = row


def far_kernel(own_aux, own_docs, oth_aux, oth_docs, own_near, oth_near, *rest):
    tables, (own_out, oth_out, total_out) = rest[:-3], rest[-3:]
    total = jnp.zeros((1, LANES), F32)
    sides = (
        (own_aux, own_docs, own_near, own_out),
        (oth_aux, oth_docs, oth_near, oth_out),
    )
    for aux, docs, near, out in sides:
        label = aux[0].astype(jnp.int32)
        for g, row in enumerate(squares(label, near, docs, tables, FAR)):
            out[g : g + 1, :] = row
            total = total + row
    total_out[...] = jnp.broadcast_to(total[None], total_out.shape)


def combine_kernel(scale, own, *rest):
    arrived, totals, out = rest[:-2], rest[-2], rest[-1]
    step = own.shape[0] - EXTRA
    share, width = out.shape[1] - EXTRA, out.shape[2]
    fold = width // 4
    sums = own[...]
    for other in arrived:
        sums = sums + other[...].astype(F32)
    inertia = jnp.sum(jnp.sum(totals[...], axis=0), axis=1, keepdims=True) * scale
    parts = jnp.concatenate(
        [jnp.broadcast_to(part, (1, fold)) for part in split3(inertia)], axis=1
    )
    for z in range(out.shape[0]):
        out[z, 0:share, :] = sums[z * share : (z + 1) * share].astype(BF16)
        row = sums[step + z : step + z + 1]
        counts = row[:, :fold]
        mass = row[:, fold : 2 * fold] + row[:, 2 * fold : 3 * fold] + row[:, 3 * fold :]
        counts_one, counts_two, _ = split3(counts)
        first = jnp.concatenate([counts_one, *split3(mass)], axis=1)
        second = jnp.concatenate([counts_two, parts], axis=1)
        pad = jnp.zeros((EXTRA - 2, width), F32)
        out[z, share:, :] = jnp.concatenate([first, second, pad], axis=0).astype(BF16)


def update_kernel(recv, old, centroids, quality, inertia):
    share, width = old.shape
    fold = width // 4
    total = recv[0].astype(F32)
    for p in range(1, recv.shape[0]):
        total = total + recv[p].astype(F32)
    first, second = total[share : share + 1], total[share + 1 : share + 2]
    counts = first[:, :fold] + second[:, :fold]
    mass = (first[:, fold : 2 * fold] + first[:, 2 * fold : 3 * fold]) + first[:, 3 * fold :]
    quality[...] = mass / (counts + 1.0)
    inertia[...] = jnp.broadcast_to(
        second[:, fold : fold + 1]
        + second[:, 2 * fold : 2 * fold + 1]
        + second[:, 3 * fold : 3 * fold + 1],
        inertia.shape,
    )
    wide = jnp.concatenate([mass, mass], axis=1)
    wide = jnp.broadcast_to(wide, (LANES, LANES)).T[:share]
    divisor = jnp.concatenate([wide] * (width // LANES), axis=1) + 1.0
    centroids[...] = ((total[:share] + old[...].astype(F32)) / divisor).astype(BF16)


def per_device(documents, assign, quality, centroids):
    rows, width = documents.shape
    y, z = lax.axis_index("y"), lax.axis_index("z")
    me = lax.axis_index("mp")
    n_mp, n_y, n_z = lax.axis_size("mp"), lax.axis_size("y"), lax.axis_size("z")
    clusters = centroids.shape[0] * n_mp
    share = clusters // (2 * n_y * n_z)
    half = clusters // 2
    groups = rows // LANES
    params = pltpu.CompilerParams(vmem_limit_bytes=32 * 1024 * 1024)
    swap = [(0, 1), (1, 0)]

    oth_docs = lax.ppermute(documents, "c", swap)
    blocks = half // n_mp // share
    own_aux, send_aux, *slices = pl.pallas_call(
        prep_kernel,
        out_shape=[jax.ShapeDtypeStruct((2, groups, LANES), F32)] * 2
        + [jax.ShapeDtypeStruct((blocks, share, width), BF16)] * n_mp,
        in_specs=[ANY, ANY, ANY],
        out_specs=[VMEM] * (2 + n_mp),
        scratch_shapes=[
            pltpu.VMEM((groups, LANES), jnp.int32),
            pltpu.VMEM((groups, LANES), F32),
            pltpu.VMEM((blocks, share, n_mp * width), BF16),
            pltpu.SemaphoreType.DMA((blocks + 2,)),
        ],
        cost_estimate=cost(0, 2 * half * width * 2),
        name="prep",
    )(
        assign.reshape(groups, LANES),
        quality.reshape(groups, LANES),
        centroids.reshape(blocks, 2, share, -1),
    )
    oth_aux = lax.ppermute(send_aux, "c", swap)
    slices = [x.reshape(half // n_mp, width) for x in slices]
    tables = [slices[0]] + [shifted(slices[s], "mp", s) for s in range(1, n_mp)]

    quarter = half // n_y
    sums = pl.pallas_call(
        scatter_kernel,
        out_shape=[jax.ShapeDtypeStruct((quarter + EXTRA, width), F32)]
        + [jax.ShapeDtypeStruct((quarter + EXTRA, width), BF16)] * (n_y - 1),
        in_specs=[VMEM] * 4,
        compiler_params=params,
        cost_estimate=cost(4 * rows * half * width, 3 * rows * width * 2),
        name="scatter",
    )(own_aux, documents, oth_aux, oth_docs)
    arrived = [shifted(sums[s], "y", s) for s in range(1, n_y)]

    own_aux, oth_aux, _ = lax.optimization_barrier((own_aux, oth_aux, sums[1]))
    near = pl.pallas_call(
        near_kernel,
        out_shape=[jax.ShapeDtypeStruct((groups, LANES), F32)] * 2,
        in_specs=[VMEM] * (4 + len(NEAR)),
        compiler_params=params,
        cost_estimate=cost(0, 0),
        name="near",
    )(own_aux, documents, oth_aux, oth_docs, *[tables[s] for s in NEAR])
    own_part, oth_part, total = pl.pallas_call(
        far_kernel,
        out_shape=[jax.ShapeDtypeStruct((groups, LANES), F32)] * 2
        + [jax.ShapeDtypeStruct((2 * n_y * n_mp, 1, LANES), F32)],
        in_specs=[VMEM] * (6 + len(FAR)),
        compiler_params=params,
        cost_estimate=cost(0, 0),
        name="far",
    )(own_aux, documents, oth_aux, oth_docs, *near, *[tables[s] for s in FAR])
    totals = all_to_all(total, ("y", "c", "mp"))
    part = own_part + lax.ppermute(oth_part, "c", swap)
    for other in [shifted(part, "mp", s) for s in range(1, n_mp)]:
        part = part + other
    distances = (part / D).reshape(rows)

    total_docs = rows * n_y * n_z * 2
    packed = pl.pallas_call(
        lambda *refs: combine_kernel(1.0 / D / total_docs, *refs),
        out_shape=jax.ShapeDtypeStruct((n_z, share + EXTRA, width), BF16),
        compiler_params=params,
        cost_estimate=cost(0, 6 * quarter * width * 2),
        name="combine",
    )(sums[0], *arrived, totals)
    recv = all_to_all(packed, "z")

    olds = [lax.dynamic_slice_in_dim(x, z * share, share, 0) for x in tables]
    source = lax.rem(me - y + n_mp, n_mp)
    old = olds[0]
    for s in range(1, n_mp):
        old = jnp.where(source == s, olds[s], old)
    new_centroids, cluster_quality, inertia = pl.pallas_call(
        update_kernel,
        out_shape=(
            jax.ShapeDtypeStruct((share, width), BF16),
            jax.ShapeDtypeStruct((1, share), F32),
            jax.ShapeDtypeStruct((1, LANES), F32),
        ),
        compiler_params=params,
        cost_estimate=cost(0, 9 * share * width * 2),
        name="update",
    )(recv, old)
    return distances, new_centroids, cluster_quality.reshape(share), inertia[0, 0]


def solution(mesh):
    n_dp, n_mp = mesh.devices.shape
    n_y, n_z = 4, n_dp // 8
    fine = Mesh(mesh.devices.reshape(n_y, n_z, 2, n_mp), ("y", "z", "c", "mp"))
    dp = ("y", "z", "c")
    return jax.shard_map(
        per_device,
        mesh=fine,
        in_specs=(P(dp, "mp"), P(dp), P(dp), P("mp", None)),
        out_specs=(P(dp), P(dp, "mp"), P(dp), P()),
        check_vma=False,
    )
```

```python
import jax
import jax.numpy as jnp
from jax import lax
from jax.experimental import pallas as pl
from jax.experimental.pallas import tpu as pltpu
from jax.sharding import Mesh, PartitionSpec as P

D = 1024
F32 = jnp.float32
BF16 = jnp.bfloat16
TILE = 256
DOCS = 512
EXTRA = 16
NEAR = (0, 1, 3)
FAR = (2,)
LANES = 128
VMEM = pl.BlockSpec(memory_space=pltpu.VMEM)
SMEM = pl.BlockSpec(memory_space=pltpu.SMEM)
ANY = pl.BlockSpec(memory_space=pl.ANY)


def all_to_all(x, axes):
    return lax.all_to_all(x, axes, split_axis=0, concat_axis=0, tiled=True)


def shifted(x, axis, step):
    size = lax.axis_size(axis)
    return lax.ppermute(x, axis, [(i, (i + step) % size) for i in range(size)])


def cost(flops, moved):
    return pl.CostEstimate(flops=flops, bytes_accessed=moved, transcendentals=0)


def split3(x):
    one = x.astype(BF16)
    rest = x - one.astype(F32)
    two = rest.astype(BF16)
    three = (rest - two.astype(F32)).astype(BF16)
    return one.astype(F32), two.astype(F32), three.astype(F32)


def placed(label, share):
    owner = lax.shift_right_logical(label, share.bit_length() - 1)
    local = lax.bitwise_and(label, share - 1)
    return lax.bitwise_and(owner, 1), lax.shift_right_logical(owner, 1) * share + local


def own_labels(assign, share):
    side, half = placed(assign[...], share)
    return jnp.where(side == lax.axis_index("c"), half, -1)


def prep_kernel(assign, quality, cents, oth_aux, *outs_and_scratch):
    outs, (label_in, weight_in, block, sems) = outs_and_scratch[:-4], outs_and_scratch[-4:]
    core, me = lax.axis_index("c"), lax.axis_index("mp")
    parts = len(outs)
    share, width = outs[0].shape[1], outs[0].shape[2]
    blocks = block.shape[0]
    copies = [
        pltpu.make_async_copy(cents.at[i, core], block.at[i], sems.at[i]) for i in range(blocks)
    ]
    small = [
        pltpu.make_async_copy(assign, label_in, sems.at[blocks]),
        pltpu.make_async_copy(quality, weight_in, sems.at[blocks + 1]),
    ]
    for copy in small + copies:
        copy.start()
    for copy in small:
        copy.wait()
    side, half = placed(label_in[...], share)
    oth_aux[0] = jnp.where(side == core, -1, half).astype(F32)
    oth_aux[1] = weight_in[...].astype(BF16).astype(F32)
    for i, copy in enumerate(copies):
        copy.wait()
        for s in range(parts):
            to = lax.rem(me + s, parts)
            columns = pl.ds(pl.multiple_of(to * width, width), width)
            outs[s][i] = block[i, :, columns]


def scatter_kernel(assign, quality, own_docs, oth_aux, oth_docs, own_sums, *sums):
    rows = own_docs.shape[0]
    quarters = len(sums) + 1
    step = own_sums.shape[0] - EXTRA
    sub = lax.broadcasted_iota(jnp.int32, (TILE, LANES), 0).astype(F32).astype(BF16)
    y = lax.axis_index("y")
    sides = []
    share = own_docs.shape[1] // 4
    own_weight = quality[...].astype(BF16).astype(F32)
    for label, weight, docs in (
        (own_labels(assign, share), own_weight, own_docs),
        (oth_aux[0].astype(jnp.int32), oth_aux[1], oth_docs),
    ):
        shift = lax.bitwise_and(
            lax.shift_right_arithmetic(label, step.bit_length() - 1) - y, quarters - 1
        )
        moved = jnp.where(label < 0, -1, shift * step + lax.bitwise_and(label, step - 1))
        sides.append((moved.astype(F32), weight, docs))

    order = list(range(1, quarters)) + [0]
    for q in order:
        out = own_sums if q == 0 else sums[q - 1]
        for t in range(step // TILE):
            base = float(q * step + t * TILE)
            total = jnp.zeros((TILE, own_docs.shape[1]), F32)
            for label, weight, docs in sides:
                rel = jnp.clip(label - base, -1.0, float(TILE)).astype(BF16)
                weight = weight.astype(BF16)
                hot = jnp.concatenate(
                    [
                        jnp.where(
                            sub == jnp.broadcast_to(rel[r : r + 1], (TILE, LANES)),
                            jnp.broadcast_to(weight[r : r + 1], (TILE, LANES)),
                            jnp.zeros((TILE, LANES), BF16),
                        )
                        for r in range(rows // LANES)
                    ],
                    axis=1,
                )
                total = total + jnp.dot(hot, docs[...], preferred_element_type=F32)
            out[t * TILE : (t + 1) * TILE, :] = total.astype(out.dtype)

    owners = quarters * step // share
    owner_sub = lax.broadcasted_iota(jnp.int32, (owners, LANES), 0).astype(F32)
    local_sub = lax.broadcasted_iota(jnp.int32, (share, LANES), 0).astype(F32)
    total = jnp.zeros((owners, 2 * share), F32)
    for label, weight, docs in sides:
        owner = jnp.floor(label * (1.0 / share))
        local = label - owner * share
        owner_hot, local_hot = [], []
        for r in range(rows // LANES):
            owner_hot.append((owner_sub == owner[r : r + 1]).astype(F32))
            same = local_sub == local[r : r + 1]
            local_hot.append(
                jnp.concatenate(
                    [same.astype(F32), jnp.where(same, weight[r : r + 1], 0.0)], axis=0
                )
            )
        total = total + lax.dot_general(
            jnp.concatenate(owner_hot, axis=1).astype(BF16),
            jnp.concatenate(local_hot, axis=1).astype(BF16),
            (((1,), (1,)), ((), ())),
            preferred_element_type=F32,
        )
    packed = jnp.concatenate([total[:, :share], *split3(total[:, share:])], axis=1)
    per = owners // quarters
    for q in order:
        out = own_sums if q == 0 else sums[q - 1]
        piece = packed[q * per : (q + 1) * per]
        pad = jnp.zeros((EXTRA - per, piece.shape[1]), F32)
        out[step:, :] = jnp.concatenate([piece, pad], axis=0).astype(out.dtype)


def squares(label, row_in, docs, tables, shifts):
    step = tables[0].shape[0]
    rows = docs.shape[0]
    per = DOCS // LANES
    parts = lax.axis_size("mp")
    lane = lax.broadcasted_iota(jnp.int32, (DOCS, TILE), 1).astype(F32).astype(BF16)
    shift = lax.bitwise_and(
        lax.axis_index("mp") - lax.shift_right_arithmetic(label, step.bit_length() - 1),
        parts - 1,
    )
    moved = jnp.full(label.shape, -1, jnp.int32)
    for k, s in enumerate(shifts):
        moved = jnp.where(shift == s, k * step + lax.bitwise_and(label, step - 1), moved)
    moved = jnp.where(label < 0, -1, moved).astype(F32)
    result = []
    for i in range(rows // DOCS):
        columns = []
        for j in range(per):
            row = moved[i * per + j : i * per + j + 1]
            columns.append(jnp.broadcast_to(row, (LANES, LANES)).T)
        column = jnp.concatenate(columns, axis=0)
        high = jnp.floor(column * (1.0 / TILE))
        low = (column - high * TILE).astype(BF16)
        high = high.astype(BF16)
        same = jnp.concatenate([low, low], axis=1) == lane
        picked = jnp.zeros((DOCS, docs.shape[1]), F32)
        for k, table in enumerate(tables):
            hots = []
            for t in range(step // TILE):
                hit = jnp.where(
                    high == jnp.full((DOCS, LANES), k * (step // TILE) + t, BF16),
                    jnp.ones((DOCS, LANES), BF16),
                    jnp.zeros((DOCS, LANES), BF16),
                )
                hots.append(
                    jnp.where(
                        same, jnp.concatenate([hit, hit], axis=1), jnp.zeros((DOCS, TILE), BF16)
                    )
                )
            picked = picked + jnp.dot(
                jnp.concatenate(hots, axis=1), table[...], preferred_element_type=F32
            )
        diff = docs[i * DOCS : (i + 1) * DOCS, :].astype(F32) - picked
        square = diff * diff
        folded = square[:, :LANES]
        for k in range(1, square.shape[1] // LANES):
            folded = folded + square[:, k * LANES : (k + 1) * LANES]
        for j in range(per):
            g = i * per + j
            row = jnp.sum(folded[j * LANES : (j + 1) * LANES].T, axis=0, keepdims=True)
            other = 0.0 if row_in is None else row_in[g : g + 1, :]
            result.append(jnp.where(moved[g : g + 1] >= 0.0, row, other))
    return result


def keep_old(out, before, tables, shifts):
    share, parts = out.shape[0], lax.axis_size("mp")
    source = lax.rem(lax.axis_index("mp") - lax.axis_index("y") + parts, parts)
    first = pl.multiple_of(lax.axis_index("z") * share, share)
    out[...] = jnp.zeros(out.shape, out.dtype) if before is None else before[...]
    for s, table in zip(shifts, tables):

        @pl.when(source == s)
        def _():
            out[...] = table[pl.ds(first, share), :]


def near_kernel(assign, own_docs, oth_aux, oth_docs, *rest):
    tables, outs, old = rest[:-3], rest[-3:-1], rest[-1]
    keep_old(old, None, tables, NEAR)
    own, oth = own_labels(assign, own_docs.shape[1] // 4), oth_aux[0].astype(jnp.int32)
    for label, docs, out in ((own, own_docs, outs[0]), (oth, oth_docs, outs[1])):
        for g, row in enumerate(squares(label, None, docs, tables, NEAR)):
            out[g : g + 1, :] = row


def far_kernel(assign, own_docs, oth_aux, oth_docs, own_near, oth_near, before, *rest):
    tables, (own_out, oth_out, total_out, old) = rest[:-4], rest[-4:]
    keep_old(old, before, tables, FAR)
    total = jnp.zeros((1, LANES), F32)
    sides = (
        (own_labels(assign, own_docs.shape[1] // 4), own_docs, own_near, own_out),
        (oth_aux[0].astype(jnp.int32), oth_docs, oth_near, oth_out),
    )
    for label, docs, near, out in sides:
        for g, row in enumerate(squares(label, near, docs, tables, FAR)):
            out[g : g + 1, :] = row
            total = total + row
    total_out[...] = jnp.broadcast_to(total[None], total_out.shape)


def combine_kernel(scale, own, *rest):
    arrived, totals, out = rest[:-2], rest[-2], rest[-1]
    step = own.shape[0] - EXTRA
    share, width = out.shape[1] - EXTRA, out.shape[2]
    fold = width // 4
    sums = own[...]
    for other in arrived:
        sums = sums + other[...].astype(F32)
    inertia = jnp.sum(jnp.sum(totals[...], axis=0), axis=1, keepdims=True) * scale
    parts = jnp.concatenate(
        [jnp.broadcast_to(part, (1, fold)) for part in split3(inertia)], axis=1
    )
    for z in range(out.shape[0]):
        out[z, 0:share, :] = sums[z * share : (z + 1) * share].astype(BF16)
        row = sums[step + z : step + z + 1]
        counts = row[:, :fold]
        mass = row[:, fold : 2 * fold] + row[:, 2 * fold : 3 * fold] + row[:, 3 * fold :]
        counts_one, counts_two, _ = split3(counts)
        first = jnp.concatenate([counts_one, *split3(mass)], axis=1)
        second = jnp.concatenate([counts_two, parts], axis=1)
        pad = jnp.zeros((EXTRA - 2, width), F32)
        out[z, share:, :] = jnp.concatenate([first, second, pad], axis=0).astype(BF16)


def update_kernel(recv, old, centroids, quality, inertia):
    share, width = old.shape
    fold = width // 4
    total = recv[0].astype(F32)
    for p in range(1, recv.shape[0]):
        total = total + recv[p].astype(F32)
    first, second = total[share : share + 1], total[share + 1 : share + 2]
    counts = first[:, :fold] + second[:, :fold]
    mass = (first[:, fold : 2 * fold] + first[:, 2 * fold : 3 * fold]) + first[:, 3 * fold :]
    quality[...] = mass / (counts + 1.0)
    inertia[...] = jnp.broadcast_to(
        second[:, fold : fold + 1]
        + second[:, 2 * fold : 2 * fold + 1]
        + second[:, 3 * fold : 3 * fold + 1],
        inertia.shape,
    )
    wide = jnp.concatenate([mass, mass], axis=1)
    wide = jnp.broadcast_to(wide, (LANES, LANES)).T[:share]
    divisor = jnp.concatenate([wide] * (width // LANES), axis=1) + 1.0
    centroids[...] = ((total[:share] + old[...].astype(F32)) / divisor).astype(BF16)


def per_device(documents, assign, quality, centroids):
    rows, width = documents.shape
    n_mp, n_y, n_z = lax.axis_size("mp"), lax.axis_size("y"), lax.axis_size("z")
    clusters = centroids.shape[0] * n_mp
    share = clusters // (2 * n_y * n_z)
    half = clusters // 2
    groups = rows // LANES
    params = pltpu.CompilerParams(vmem_limit_bytes=32 * 1024 * 1024)
    swap = [(0, 1), (1, 0)]

    oth_docs = lax.ppermute(documents, "c", swap)
    blocks = half // n_mp // share
    assign = assign.reshape(groups, LANES)
    quality = quality.reshape(groups, LANES)
    send_aux, *slices = pl.pallas_call(
        prep_kernel,
        out_shape=[jax.ShapeDtypeStruct((2, groups, LANES), F32)]
        + [jax.ShapeDtypeStruct((blocks, share, width), BF16)] * n_mp,
        in_specs=[ANY, ANY, ANY],
        out_specs=[VMEM] * (1 + n_mp),
        scratch_shapes=[
            pltpu.VMEM((groups, LANES), jnp.int32),
            pltpu.VMEM((groups, LANES), F32),
            pltpu.VMEM((blocks, share, n_mp * width), BF16),
            pltpu.SemaphoreType.DMA((blocks + 2,)),
        ],
        cost_estimate=cost(0, 2 * half * width * 2),
        name="prep",
    )(
        assign,
        quality,
        centroids.reshape(blocks, 2, share, -1),
    )
    oth_aux = lax.ppermute(send_aux, "c", swap)
    slices = [x.reshape(half // n_mp, width) for x in slices]

    quarter = half // n_y
    sums = pl.pallas_call(
        scatter_kernel,
        out_shape=[jax.ShapeDtypeStruct((quarter + EXTRA, width), F32)]
        + [jax.ShapeDtypeStruct((quarter + EXTRA, width), BF16)] * (n_y - 1),
        in_specs=[VMEM] * 5,
        compiler_params=params,
        cost_estimate=cost(4 * rows * half * width, 3 * rows * width * 2),
        name="scatter",
    )(assign, quality, documents, oth_aux, oth_docs)
    slices[2], _ = lax.optimization_barrier((slices[2], sums[1]))
    tables = [slices[0]] + [shifted(slices[s], "mp", s) for s in range(1, n_mp)]

    oth_aux, _ = lax.optimization_barrier((oth_aux, sums[1]))
    near = pl.pallas_call(
        near_kernel,
        out_shape=[jax.ShapeDtypeStruct((groups, LANES), F32)] * 2
        + [jax.ShapeDtypeStruct((share, width), BF16)],
        in_specs=[VMEM] * (4 + len(NEAR)),
        compiler_params=params,
        cost_estimate=cost(0, 0),
        name="near",
    )(assign, documents, oth_aux, oth_docs, *[tables[s] for s in NEAR])
    *moving, near = lax.optimization_barrier((*sums[1:], near))
    arrived = [shifted(x, "y", s + 1) for s, x in enumerate(moving)]
    own_part, oth_part, total, old = pl.pallas_call(
        far_kernel,
        out_shape=[jax.ShapeDtypeStruct((groups, LANES), F32)] * 2
        + [
            jax.ShapeDtypeStruct((2 * n_y * n_mp, 1, LANES), F32),
            jax.ShapeDtypeStruct((share, width), BF16),
        ],
        in_specs=[VMEM] * (7 + len(FAR)),
        compiler_params=params,
        cost_estimate=cost(0, 0),
        name="far",
    )(assign, documents, oth_aux, oth_docs, *near, *[tables[s] for s in FAR])
    totals = all_to_all(total, ("y", "c", "mp"))
    part = own_part + lax.ppermute(oth_part, "c", swap)
    for other in [shifted(part, "mp", s) for s in range(1, n_mp)]:
        part = part + other
    distances = (part / D).reshape(rows)

    total_docs = rows * n_y * n_z * 2
    packed = pl.pallas_call(
        lambda *refs: combine_kernel(1.0 / D / total_docs, *refs),
        out_shape=jax.ShapeDtypeStruct((n_z, share + EXTRA, width), BF16),
        compiler_params=params,
        cost_estimate=cost(0, 6 * quarter * width * 2),
        name="combine",
    )(sums[0], *arrived, totals)
    recv = all_to_all(packed, "z")

    new_centroids, cluster_quality, inertia = pl.pallas_call(
        update_kernel,
        out_shape=(
            jax.ShapeDtypeStruct((share, width), BF16),
            jax.ShapeDtypeStruct((1, share), F32),
            jax.ShapeDtypeStruct((1, LANES), F32),
        ),
        compiler_params=params,
        cost_estimate=cost(0, 9 * share * width * 2),
        name="update",
    )(recv, old)
    return distances, new_centroids, cluster_quality.reshape(share), inertia[0, 0]


def solution(mesh):
    n_dp, n_mp = mesh.devices.shape
    n_y, n_z = 4, n_dp // 8
    fine = Mesh(mesh.devices.reshape(n_y, n_z, 2, n_mp), ("y", "z", "c", "mp"))
    dp = ("y", "z", "c")
    return jax.shard_map(
        per_device,
        mesh=fine,
        in_specs=(P(dp, "mp"), P(dp), P(dp), P("mp", None)),
        out_specs=(P(dp), P(dp, "mp"), P(dp), P()),
        check_vma=False,
    )
```
